32 devices in a mesh: wide: 16 (over z, y, x), narrow: 2 (over core).
Axes of the slice: x: 2, y: 2, z: 4, core: 2. Of those that a mesh axis runs over, the one named last changes fastest.
Arguments:
- hidden: bfloat16 [512, 8192], P('wide', 'narrow'), may hold values from -6 to 6
- norm_gain: float32 [8192], P('narrow'), may hold values from 0.1 to 1.9
- head_weight: bfloat16 [8192, 32000], P('narrow', 'wide'), may hold values from -0.24 to 0.24
- diff_rows: bfloat16 [16, 2, 8, 32000], P('wide', 'narrow'), may hold values from -6 to 480
- slot_request: int32 [16, 2, 8], replicated, may hold values from 0 to 511, as said below
- slot_code: int32 [16, 2, 8], replicated, may hold values from 1 to 8
- slot_count: int32 [16, 2], replicated, may hold values from 1 to 8, as said below
Outputs:
- log_probs: float32 [512, 32000], P('narrow', 'wide')
The draws below stay inside these ranges and needn't reach their ends.
Inputs may be any that keep to these rules, and one draw needn't show every extreme that they name: `slot_request`: within one pair, every request is named at most once. `slot_count`: slots at or beyond the count hold no row to use; in every draw some device uses all 8 slots.
All inputs are finite; a program needn't handle non-finite values.
Results may differ from the reference program's by a relative error of at most 0.0003.
Values may be sent and summed in bfloat16 or wider, within the bound.
No kernel may reach another device: no remote copies, remote signals or barrier semaphores. Data moves between devices by JAX's collectives and lax.ppermute only.
A program may use at most 64 MiB of HBM per device.

```python
import jax
import jax.numpy as jnp
from jax import lax

D = 8192
VOCAB = 32000
REQ_DEV = 32
CAP = 8
REQUESTS = 512
PAIRS = 16
N_WIDE = 16
N_NARROW = 2


def state_values(key):
    return jnp.clip(jax.random.normal(jax.random.fold_in(key, 11), (REQUESTS, D), jnp.float32), -6.0, 6.0)


def draw_hidden(key, part):
    return state_values(key).astype(jnp.bfloat16)


def draw_head_weight(key, part):
    key_weight = jax.random.fold_in(key, 23)
    return jnp.clip(0.04 * jax.random.normal(key_weight, (D, VOCAB), jnp.float32), -0.24, 0.24).astype(jnp.bfloat16)


def draw_diff_rows(key, part):
    key_values = jax.random.fold_in(key, 0)
    shape = (N_WIDE, N_NARROW, CAP, VOCAB)
    return jnp.clip(jax.random.normal(key_values, shape, jnp.float32), -6.0, 6.0).astype(jnp.bfloat16)


def permute(pair_key):
    return jax.random.permutation(pair_key, REQ_DEV * N_WIDE)[:N_NARROW * CAP]


def draw_slot_request(key, part):
    total = REQ_DEV * N_WIDE
    pair_keys = jax.random.split(key, N_WIDE)
    orders = jax.vmap(permute)(pair_keys).astype(jnp.int32)
    groups = jnp.arange(N_WIDE, dtype=jnp.int32)[:, None]
    target = jnp.where(groups == 0, total - 1, jnp.where(groups == 1, 0, orders[:, :1]))
    chosen = (orders + target - orders[:, :1]) % total
    return chosen.reshape(N_WIDE, N_NARROW, CAP).astype(jnp.int32)


def draw_slot_count(key, part):
    key_first, key_second, key_full = jax.random.split(key, 3)
    first_draw = jax.random.randint(key_first, (N_WIDE, N_NARROW), 0, CAP)
    second_draw = jax.random.randint(key_second, (N_WIDE, N_NARROW), 0, CAP)
    divisor = max(1, CAP // 2)
    counts = jnp.minimum(CAP, 1 + first_draw * second_draw // divisor).reshape(-1)
    full_slot = jax.random.randint(key_full, (), 0, N_WIDE * N_NARROW)
    counts = jnp.where(jnp.arange(N_WIDE * N_NARROW, dtype=jnp.int32) == full_slot, CAP, counts)
    return counts.reshape(N_WIDE, N_NARROW).astype(jnp.int32)


def touch_ends(drawn, key, smallest, high):
    longest = drawn.shape.index(max(drawn.shape))
    spots = []
    for shift in (0, 1):
        where = [jax.random.randint(jax.random.fold_in(key, axis), (), 0, length) for axis, length in enumerate(drawn.shape)]
        where[longest] = (where[longest] + shift) % drawn.shape[longest]
        spots.append(tuple(where))
    return drawn.at[spots[0]].set(smallest).at[spots[1]].set(high)


def setup_inputs(seed: int = 0) -> dict:
    keys = jax.random.split(jax.random.key(seed), 8)
    hidden = draw_hidden(jax.random.fold_in(keys[7], 71), 0)
    norm_gain = jnp.clip(1.0 + 0.18 * jax.random.normal(keys[1], (D,), jnp.float32), 0.1, 1.9)
    head_weight = draw_head_weight(jax.random.fold_in(keys[7], 71), 0)
    diff_rows = draw_diff_rows(jax.random.fold_in(keys[7], 71), 0)
    slot_request = draw_slot_request(jax.random.fold_in(keys[7], 71), 0)
    slot_code = touch_ends(jax.random.randint(keys[5], (PAIRS, N_NARROW, CAP), 1, 9), jax.random.fold_in(keys[5], 1), 1, 8).astype(jnp.int32)
    slot_count = draw_slot_count(jax.random.fold_in(keys[7], 71), 0)
    return dict(hidden=hidden, norm_gain=norm_gain, head_weight=head_weight, diff_rows=diff_rows, slot_request=slot_request, slot_code=slot_code, slot_count=slot_count)


epsilon = 1e-05

def reference(hidden, norm_gain, head_weight, diff_rows, slot_request, slot_code, slot_count):
    values = hidden.astype(jnp.float32)
    scales = lax.rsqrt(lax.optimization_barrier(jnp.mean(values * values, axis=1, keepdims=True)) + epsilon)
    normed = (values * scales * norm_gain[None, :]).astype(jnp.bfloat16)
    logits = jnp.dot(normed, head_weight, preferred_element_type=jnp.float32)
    active = jnp.arange(CAP, dtype=jnp.int32)[None, None, :] < slot_count[:, :, None]
    factors = jnp.where(active, slot_code, 0).astype(jnp.float32) * 0.25

    def add_group(running, element):
        row_block, requests, weights = element
        weighted = row_block.reshape(-1, VOCAB).astype(jnp.float32) * weights.reshape(-1)[:, None]
        return (running.at[requests.reshape(-1)].add(weighted), None)
    logits, _ = lax.scan(add_group, logits, (diff_rows, slot_request, factors))
    row_peak = lax.optimization_barrier(jnp.max(logits, axis=1, keepdims=True))
    log_total = row_peak + jnp.log(lax.optimization_barrier(jnp.sum(jnp.exp(logits - row_peak), axis=1, keepdims=True)))
    return logits - log_total
```

```python
import jax
import jax.numpy as jnp
from jax import lax
from jax.experimental import pallas as pl
from jax.experimental.pallas import tpu as pltpu
from jax.sharding import PartitionSpec as P

D = 8192


epsilon = 1e-05


def flip(a, axis, mask):
    size = lax.axis_size(axis)
    return lax.ppermute(a, axis, [(i, i ^ mask) for i in range(size)])


def after(a, *others):
    return lax.optimization_barrier((a, *others))[0]


def normalise(hidden, norm_gain):
    values = hidden.astype(jnp.float32)
    sums = jnp.sum(values * values, axis=1)
    squares = sums + flip(sums, "narrow", 1)
    scales = lax.rsqrt(squares / D + epsilon)
    return (values * scales[:, None] * norm_gain[None, :]).astype(jnp.bfloat16)


def vocabulary_slices(row_block, parts):
    def kernel(rows_ref, slices_ref):
        width = slices_ref.shape[2]
        for part in range(parts):
            slices_ref[part] = rows_ref[:, part * width : (part + 1) * width]

    slots, vocabulary = row_block.shape
    return pl.pallas_call(
        kernel,
        out_shape=jax.ShapeDtypeStruct((parts, slots, vocabulary // parts), row_block.dtype),
        cost_estimate=pl.CostEstimate(flops=0, bytes_accessed=4 * slots * vocabulary, transcendentals=0),
        name="vocabulary_slices",
    )(row_block)


def tile_of(length):
    return max(t for t in range(16, 513, 16) if length % t == 0)


ANYWHERE = pl.BlockSpec(memory_space=pl.ANY)
SCALAR = pl.BlockSpec(memory_space=pltpu.SMEM)
ROOM = pltpu.CompilerParams(vmem_limit_bytes=56 * 2**20)


def every(count, step):
    def loop(i, _):
        step(i)
        return 0

    lax.fori_loop(0, count, loop, 0)


def rows_at(i, tile):
    return pl.ds(pl.multiple_of(i * tile, 8), tile)


def multiply(blocks, weight_t, first, diffs_t, mixing, begin=0, end=None, into=None):
    vocabulary, width = weight_t.shape
    count, rows = len(blocks), blocks[0].shape[0]
    slots = diffs_t.shape[1]
    tile = tile_of(vocabulary)
    end = vocabulary // tile if end is None else end
    chunks = end - begin
    contract_last = (((1,), (1,)), ((), ()))

    def kernel(first_ref, *refs):
        block_refs, refs = refs[:count], refs[count:]
        if into is not None:
            refs = refs[1:]
        weight_hbm, diffs_hbm, mixing_hbm, out_hbm, states, weight, diffs, mixed, out = refs[:9]
        state_sems, weight_sems, side_sems, out_sems = refs[9:]

        def weight_copy(chunk):
            place = rows_at(begin + chunk, tile)
            return pltpu.make_async_copy(weight_hbm.at[place], weight.at[place], weight_sems.at[chunk])

        def out_copy(chunk):
            place = rows_at(begin + chunk, tile)
            return pltpu.make_async_copy(out.at[place], out_hbm.at[place], out_sems.at[chunk])

        def add_chunk(chunk):
            weight_copy(chunk).wait()
            place = rows_at(begin + chunk, tile)
            out[place, :] = lax.dot_general(
                weight[place, :], states[...], contract_last, preferred_element_type=jnp.float32
            ) + lax.dot_general(diffs[place, :], mixed[...], contract_last, preferred_element_type=jnp.float32)
            out_copy(chunk).start()

        first_copies = [
            pltpu.make_async_copy(
                block_refs[k],
                states.at[pl.ds(pl.multiple_of((first_ref[0] ^ k) * rows, rows), rows)],
                state_sems.at[k],
            )
            for k in range(count)
        ]
        first_copies.append(pltpu.make_async_copy(diffs_hbm, diffs, side_sems.at[0]))
        first_copies.append(pltpu.make_async_copy(mixing_hbm, mixed, side_sems.at[1]))
        for copy in first_copies:
            copy.start()
        every(chunks, lambda chunk: weight_copy(chunk).start())
        for copy in first_copies:
            copy.wait()
        every(chunks, add_chunk)
        every(chunks, lambda chunk: out_copy(chunk).wait())

    held = [] if into is None else [into]
    return pl.pallas_call(
        kernel,
        in_specs=[SCALAR] + [ANYWHERE] * (count + 3 + len(held)),
        out_specs=ANYWHERE,
        out_shape=jax.ShapeDtypeStruct((vocabulary, count * rows), jnp.float32),
        scratch_shapes=[
            pltpu.VMEM((count * rows, width), jnp.bfloat16),
            pltpu.VMEM((vocabulary, width), jnp.bfloat16),
            pltpu.VMEM((vocabulary, slots), jnp.bfloat16),
            pltpu.VMEM((count * rows, slots), jnp.bfloat16),
            pltpu.VMEM((vocabulary, count * rows), jnp.float32),
            pltpu.SemaphoreType.DMA((count,)),
            pltpu.SemaphoreType.DMA((chunks,)),
            pltpu.SemaphoreType.DMA((2,)),
            pltpu.SemaphoreType.DMA((chunks,)),
        ],
        compiler_params=ROOM,
        cost_estimate=pl.CostEstimate(
            flops=2 * chunks * tile * width * count * rows, bytes_accessed=2 * chunks * tile * width, transcendentals=0
        ),
        input_output_aliases={1 + count: 0} if held else {},
        name="multiply",
    )(first.reshape(1), *blocks, *held, weight_t, diffs_t, mixing)


def statistics(near, near_other, far, far_other, late, parts):
    vocabulary, rows = near.shape
    tile = tile_of(vocabulary)
    chunks = vocabulary // tile

    def kernel(late_ref, near_ref, near_other_ref, far_ref, far_other_ref, total_hbm, stats_ref, left, right, *sems):
        left_sems, right_sems, out_sems = sems

        def fetch(chunk, left_side, right_side):
            place = rows_at(chunk, tile)
            return [
                pltpu.make_async_copy(left_side.at[place], left.at[place], left_sems.at[chunk]),
                pltpu.make_async_copy(right_side.at[place], right.at[place], right_sems.at[chunk]),
            ]

        def out_copy(chunk):
            place = rows_at(chunk, tile)
            return pltpu.make_async_copy(left.at[place], total_hbm.at[place], out_sems.at[chunk])

        def start_all(left_side, right_side):
            def start(chunk):
                for copy in fetch(chunk, left_side, right_side):
                    copy.start()

            every(chunks, start)

        @pl.when(late_ref[0] == 0)
        def _():
            start_all(near_ref, near_other_ref)

        @pl.when(late_ref[0] == 1)
        def _():
            start_all(far_ref, far_other_ref)

        def step(chunk, state):
            for copy in fetch(chunk, far_ref, far_other_ref):
                copy.wait()
            place = rows_at(chunk, tile)
            total = left[place, :] + right[place, :]
            left[place, :] = total
            out_copy(chunk).start()
            before, mass = state
            peak = jnp.maximum(before, jnp.max(total, axis=0, keepdims=True))
            total = left[place, :]
            mass = mass * jnp.exp(before - peak) + jnp.sum(jnp.exp(total - peak), axis=0, keepdims=True)
            return peak, mass

        state = (jnp.full((1, rows), -jnp.inf, jnp.float32), jnp.zeros((1, rows), jnp.float32))
        both = jnp.concatenate(lax.fori_loop(0, chunks, step, state))
        stats_ref[...] = jnp.broadcast_to(both[None], stats_ref.shape)
        every(chunks, lambda chunk: out_copy(chunk).wait())

    return pl.pallas_call(
        kernel,
        in_specs=[SCALAR] + [ANYWHERE] * 4,
        out_specs=[ANYWHERE, pl.BlockSpec(memory_space=pltpu.VMEM)],
        out_shape=[
            jax.ShapeDtypeStruct((vocabulary, rows), jnp.float32),
            jax.ShapeDtypeStruct((parts, 2, rows), jnp.float32),
        ],
        scratch_shapes=[pltpu.VMEM((vocabulary, rows), jnp.float32)] * 2 + [pltpu.SemaphoreType.DMA((chunks,))] * 3,
        compiler_params=ROOM,
        cost_estimate=pl.CostEstimate(
            flops=4 * vocabulary * rows, bytes_accessed=16 * vocabulary * rows, transcendentals=vocabulary * rows
        ),
        name="statistics",
    )(late.reshape(1), near, near_other, far, far_other)


def subtract(total, arrived):
    vocabulary, rows = total.shape
    tile = tile_of(vocabulary)
    chunks = vocabulary // tile

    def kernel(total_hbm, arrived_ref, out_hbm, held, in_sems, out_sems):
        def in_copy(chunk):
            place = rows_at(chunk, tile)
            return pltpu.make_async_copy(total_hbm.at[place], held.at[place], in_sems.at[chunk])

        def out_copy(chunk):
            place = rows_at(chunk, tile)
            return pltpu.make_async_copy(held.at[place], out_hbm.at[place], out_sems.at[chunk])

        every(chunks, lambda chunk: in_copy(chunk).start())
        peaks, masses = arrived_ref[:, 0, :], arrived_ref[:, 1, :]
        row_peak = jnp.max(peaks, axis=0, keepdims=True)
        row_mass = jnp.sum(masses * jnp.exp(peaks - row_peak), axis=0, keepdims=True)
        log_total = row_peak + jnp.log(row_mass)

        def shift(chunk):
            in_copy(chunk).wait()
            place = rows_at(chunk, tile)
            held[place, :] = held[place, :] - log_total
            out_copy(chunk).start()

        every(chunks, shift)
        every(chunks, lambda chunk: out_copy(chunk).wait())

    return pl.pallas_call(
        kernel,
        in_specs=[ANYWHERE, pl.BlockSpec(memory_space=pltpu.VMEM)],
        out_specs=ANYWHERE,
        out_shape=jax.ShapeDtypeStruct((vocabulary, rows), jnp.float32),
        scratch_shapes=[pltpu.VMEM((vocabulary, rows), jnp.float32)] + [pltpu.SemaphoreType.DMA((chunks,))] * 2,
        compiler_params=ROOM,
        cost_estimate=pl.CostEstimate(flops=vocabulary * rows, bytes_accessed=8 * vocabulary * rows, transcendentals=0),
        name="subtract",
    )(total, arrived)


def slot_factors(slot_code, slot_count):
    slots = slot_code.shape[2]
    active = jnp.arange(slots, dtype=jnp.int32)[None, None, :] < slot_count[:, :, None]
    return jnp.where(active, slot_code, 0).astype(jnp.float32) * 0.25


def body(hidden, norm_gain, head_weight, diff_rows, slot_request, slot_code, slot_count):
    me, core = lax.axis_index("wide"), lax.axis_index("narrow")
    parts, rows = lax.axis_size("wide"), hidden.shape[0]
    weight_t = head_weight.T

    own = normalise(hidden, norm_gain)

    row_block = diff_rows[0, 0]
    x0, y0, z1 = flip(own, "wide", 1), flip(own, "wide", 2), flip(own, "wide", 4)
    slices = vocabulary_slices(after(row_block, own), parts)
    diffs = lax.all_to_all(slices, "wide", split_axis=0, concat_axis=0, tiled=True).reshape(-1, weight_t.shape[0])
    diffs_t = diffs.T

    own, x0, y0, z1 = lax.optimization_barrier((own, x0, y0, z1))
    d0, y1, x1, z2 = flip(y0, "wide", 1), flip(z1, "wide", 2), flip(x0, "wide", 4), flip(own, "wide", 8)
    d1 = flip(x1, "wide", 2)
    z2, d0, y1, x1 = lax.optimization_barrier((z2, d0, y1, x1))
    x2, y2, z3 = flip(z2, "wide", 1), flip(z2, "wide", 2), flip(z2, "wide", 4)
    x2, y2, z3, d1 = lax.optimization_barrier((x2, y2, z3, d1))
    x3, y3 = flip(z3, "wide", 1), flip(z3, "wide", 2)

    first, half = me & 7, me // 8
    late = half ^ core
    factors = lax.dynamic_index_in_dim(slot_factors(slot_code, slot_count), core, 1, False).reshape(-1)
    targets = lax.dynamic_index_in_dim(slot_request, core, 1, False).reshape(-1)

    def mixing(which):
        requests = which * 8 * rows + jnp.arange(8 * rows, dtype=jnp.int32)
        return jnp.where(requests[:, None] == targets, factors, 0.0).astype(jnp.bfloat16)

    blocks = [own, x0, y0, d0, z1, x1, y1, d1]
    near = multiply(blocks, weight_t, first, diffs_t, mixing(half), 0, 3)
    x3, y3, y2, near = lax.optimization_barrier((x3, y3, y2, near))
    d2, d3 = flip(y2, "wide", 1), flip(x3, "wide", 2)
    near = multiply(blocks, weight_t, first, diffs_t, mixing(half), 3, 5, near)
    d2, d3, near = lax.optimization_barrier((d2, d3, near))
    near_other = flip(near, "narrow", 1)
    far = multiply([z2, x2, y2, d2, z3, x3, y3, d3], weight_t, first, diffs_t, mixing(1 - half))
    far_other = flip(far, "narrow", 1)
    total, stats = statistics(near, near_other, far, far_other, late, parts)
    arrived = lax.all_to_all(stats, "wide", split_axis=0, concat_axis=0, tiled=True)
    return subtract(total, arrived).T


def combined_all(part, axis, combine):
    gathered = jax.tree.map(lambda a: lax.all_gather(a, axis), part)

    def take(source):
        return jax.tree.map(lambda a: lax.dynamic_index_in_dim(a, source, 0, False), gathered)

    return lax.fori_loop(
        1, lax.axis_size(axis), lambda source, state: combine(state, take(source)), take(0)
    )


def merge_pair(earlier, later):
    row_peak = jnp.maximum(earlier[0], later[0])
    summed = earlier[1] * jnp.exp(earlier[0] - row_peak) + later[1] * jnp.exp(later[0] - row_peak)
    return (row_peak, summed)


def general_body(hidden, norm_gain, head_weight, diff_rows, slot_request, slot_code, slot_count):
    values = hidden.astype(jnp.float32)
    squares = lax.psum(jnp.sum(values * values, axis=1), "narrow")
    scales = lax.rsqrt(squares / D + epsilon)
    normed = (values * scales[:, None] * norm_gain[None, :]).astype(jnp.bfloat16)
    partial_value = jnp.dot(
        lax.all_gather(normed, "wide", axis=0, tiled=True),
        head_weight,
        preferred_element_type=jnp.float32,
    )
    arrived = lax.all_to_all(diff_rows[0, 0], "wide", split_axis=1, concat_axis=0, tiled=True)
    base_block = lax.psum_scatter(partial_value, "narrow", scatter_dimension=0, tiled=True)
    owner_slices = lax.all_gather(arrived, "narrow", axis=0, tiled=True)
    targets = jnp.transpose(slot_request, (1, 0, 2)).reshape(-1)
    factor_all = jnp.transpose(slot_factors(slot_code, slot_count), (1, 0, 2)).reshape(-1)
    block_rows = base_block.shape[0]
    offsets = targets - lax.axis_index("narrow") * block_rows
    owned = (offsets >= 0) & (offsets < block_rows)
    factors = jnp.where(owned, factor_all, 0.0)
    target_rows = jnp.where(owned, offsets, 0)
    own_block = base_block.at[target_rows].add(owner_slices.astype(jnp.float32) * factors[:, None])
    local_peak = jnp.max(own_block, axis=1)
    local_mass = jnp.sum(jnp.exp(own_block - local_peak[:, None]), axis=1)
    row_peak, row_mass = combined_all((local_peak, local_mass), "wide", merge_pair)
    log_total = row_peak + jnp.log(row_mass)
    return own_block - log_total[:, None]


def solution(mesh):
    placed = (
        P("wide", "narrow"),
        P("narrow"),
        P("narrow", "wide"),
        P("wide", "narrow", None, None),
        P(),
        P(),
        P(),
    )
    small = mesh.shape["wide"] == 16 and mesh.shape["narrow"] == 2
    return jax.shard_map(
        body if small else general_body,
        mesh=mesh,
        in_specs=placed,
        out_specs=P("narrow", "wide"),
        check_vma=False,
    )
```

```python
import jax
import jax.numpy as jnp
from jax import lax
from jax.experimental import pallas as pl
from jax.experimental.pallas import tpu as pltpu
from jax.sharding import PartitionSpec as P

D = 8192


epsilon = 1e-05
ANYWHERE = pl.BlockSpec(memory_space=pl.ANY)
SCALAR = pl.BlockSpec(memory_space=pltpu.SMEM)
ROOM = pltpu.CompilerParams(vmem_limit_bytes=56 * 2**20)


def flip(a, axis, mask):
    size = lax.axis_size(axis)
    return lax.ppermute(a, axis, [(i, i ^ mask) for i in range(size)])


def after(a, *others):
    return lax.optimization_barrier((a, *others))[0]


def normalise(hidden, norm_gain):
    values = hidden.astype(jnp.float32)
    sums = jnp.sum(values * values, axis=1)
    squares = sums + flip(sums, "narrow", 1)
    scales = lax.rsqrt(squares / D + epsilon)
    return (values * scales[:, None] * norm_gain[None, :]).astype(jnp.bfloat16)


def vocabulary_slices(row_block, parts):
    def kernel(rows_ref, slices_ref):
        width = slices_ref.shape[2]
        for part in range(parts):
            slices_ref[part] = rows_ref[:, part * width : (part + 1) * width]

    slots, vocabulary = row_block.shape
    return pl.pallas_call(
        kernel,
        out_shape=jax.ShapeDtypeStruct((parts, slots, vocabulary // parts), row_block.dtype),
        cost_estimate=pl.CostEstimate(flops=0, bytes_accessed=4 * slots * vocabulary, transcendentals=0),
        name="vocabulary_slices",
    )(row_block)


def tile_of(length):
    return max(t for t in range(16, 513, 16) if length % t == 0)


def every(count, step):
    def loop(i, _):
        step(i)
        return 0

    lax.fori_loop(0, count, loop, 0)


def rows_at(i, tile):
    return pl.ds(pl.multiple_of(i * tile, 8), tile)


def multiply(blocks, weight_t, first, begin, end):
    width = weight_t.shape[1]
    count, rows = len(blocks), blocks[0].shape[0]
    tile = tile_of(weight_t.shape[0])
    chunks = end - begin
    contract_last = (((1,), (1,)), ((), ()))

    def kernel(first_ref, *refs):
        block_refs, refs = refs[:count], refs[count:]
        weight_hbm, out_hbm, states, weight, out, state_sems, weight_sems, out_sems = refs

        def weight_copy(chunk):
            source = weight_hbm.at[rows_at(begin + chunk, tile)]
            return pltpu.make_async_copy(source, weight.at[rows_at(chunk, tile)], weight_sems.at[chunk])

        def out_copy(chunk):
            place = rows_at(chunk, tile)
            return pltpu.make_async_copy(out.at[place], out_hbm.at[place], out_sems.at[chunk])

        def one_chunk(chunk):
            weight_copy(chunk).wait()
            place = rows_at(chunk, tile)
            out[place, :] = lax.dot_general(
                weight[place, :], states[...], contract_last, preferred_element_type=jnp.float32
            )
            out_copy(chunk).start()

        state_copies = [
            pltpu.make_async_copy(
                block_refs[k],
                states.at[pl.ds(pl.multiple_of((first_ref[0] ^ k) * rows, rows), rows)],
                state_sems.at[k],
            )
            for k in range(count)
        ]
        for copy in state_copies:
            copy.start()
        every(chunks, lambda chunk: weight_copy(chunk).start())
        for copy in state_copies:
            copy.wait()
        every(chunks, one_chunk)
        every(chunks, lambda chunk: out_copy(chunk).wait())

    return pl.pallas_call(
        kernel,
        in_specs=[SCALAR] + [ANYWHERE] * (count + 1),
        out_specs=ANYWHERE,
        out_shape=jax.ShapeDtypeStruct((chunks * tile, count * rows), jnp.float32),
        scratch_shapes=[
            pltpu.VMEM((count * rows, width), jnp.bfloat16),
            pltpu.VMEM((chunks * tile, width), jnp.bfloat16),
            pltpu.VMEM((chunks * tile, count * rows), jnp.float32),
            pltpu.SemaphoreType.DMA((count,)),
            pltpu.SemaphoreType.DMA((chunks,)),
            pltpu.SemaphoreType.DMA((chunks,)),
        ],
        compiler_params=ROOM,
        cost_estimate=pl.CostEstimate(
            flops=8 * chunks * tile * width * count * rows, bytes_accessed=8 * chunks * tile * width, transcendentals=0
        ),
        name="multiply",
    )(first.reshape(1), *blocks, weight_t)


def statistics(near, near_other, far, far_other, diffs, mixing, late, parts):
    vocabulary, rows = far.shape
    slots = diffs[0].shape[1]
    tile = tile_of(vocabulary)
    chunks = vocabulary // tile
    pieces = len(near)
    contract_last = (((1,), (1,)), ((), ()))

    def kernel(late_ref, *refs):
        near_refs, near_other_refs, refs = refs[:pieces], refs[pieces : 2 * pieces], refs[2 * pieces :]
        far_ref, far_other_ref, *refs = refs
        diff_refs, mixing_refs, refs = refs[:2], refs[2:4], refs[4:]
        total_hbm, stats_ref, left, right, rows_in, mixed, left_sems, right_sems, out_sems, side_sems = refs

        def fetch(chunk, source, left_side, right_side):
            origin, place = rows_at(source, tile), rows_at(chunk, tile)
            return [
                pltpu.make_async_copy(left_side.at[origin], left.at[place], left_sems.at[chunk]),
                pltpu.make_async_copy(right_side.at[origin], right.at[place], right_sems.at[chunk]),
            ]

        def out_copy(chunk):
            place = rows_at(chunk, tile)
            return pltpu.make_async_copy(left.at[place], total_hbm.at[place], out_sems.at[chunk])

        def start_all(first, left_side, right_side):
            def start(chunk):
                for copy in fetch(first + chunk, chunk, left_side, right_side):
                    copy.start()

            every(left_side.shape[0] // tile, start)

        side_copies = [
            pltpu.make_async_copy(source, into.at[n], side_sems.at[side, n])
            for side, (sources, into) in enumerate(((mixing_refs, mixed), (diff_refs, rows_in)))
            for n, source in enumerate(sources)
        ]
        for copy in side_copies:
            copy.start()

        @pl.when(late_ref[0] == 0)
        def _():
            first = 0
            for left_side, right_side in zip(near_refs, near_other_refs):
                start_all(first, left_side, right_side)
                first += left_side.shape[0] // tile

        @pl.when(late_ref[0] == 1)
        def _():
            start_all(0, far_ref, far_other_ref)

        for copy in side_copies:
            copy.wait()

        def step(chunk, state):
            for copy in fetch(chunk, chunk, far_ref, far_other_ref):
                copy.wait()
            place = rows_at(chunk, tile)
            total = left[place, :] + right[place, :]
            for n in range(2):
                total += lax.dot_general(
                    rows_in[n, place, :], mixed[n], contract_last, preferred_element_type=jnp.float32
                )
            left[place, :] = total
            out_copy(chunk).start()
            before, mass = state
            peak = jnp.maximum(before, jnp.max(total, axis=0, keepdims=True))
            total = left[place, :]
            mass = mass * jnp.exp(before - peak) + jnp.sum(jnp.exp(total - peak), axis=0, keepdims=True)
            return peak, mass

        state = (jnp.full((1, rows), -jnp.inf, jnp.float32), jnp.zeros((1, rows), jnp.float32))
        both = jnp.concatenate(lax.fori_loop(0, chunks, step, state))
        stats_ref[...] = jnp.broadcast_to(both[None], stats_ref.shape)
        every(chunks, lambda chunk: out_copy(chunk).wait())

    return pl.pallas_call(
        kernel,
        in_specs=[SCALAR] + [ANYWHERE] * (2 * pieces + 6),
        out_specs=[ANYWHERE, pl.BlockSpec(memory_space=pltpu.VMEM)],
        out_shape=[
            jax.ShapeDtypeStruct((vocabulary, rows), jnp.float32),
            jax.ShapeDtypeStruct((parts, 2, rows), jnp.float32),
        ],
        scratch_shapes=[pltpu.VMEM((vocabulary, rows), jnp.float32)] * 2
        + [pltpu.VMEM((2, vocabulary, slots), jnp.bfloat16), pltpu.VMEM((2, rows, slots), jnp.bfloat16)]
        + [pltpu.SemaphoreType.DMA((chunks,))] * 3
        + [pltpu.SemaphoreType.DMA((2, 2))],
        compiler_params=ROOM,
        cost_estimate=pl.CostEstimate(
            flops=4 * vocabulary * rows, bytes_accessed=16 * vocabulary * rows, transcendentals=vocabulary * rows
        ),
        name="statistics",
    )(late.reshape(1), *near, *near_other, far, far_other, *diffs, *mixing)


def subtract(total, arrived):
    vocabulary, rows = total.shape
    tile = tile_of(vocabulary)
    chunks = vocabulary // tile

    def kernel(total_hbm, arrived_hbm, out_hbm, held, arrived_ref, in_sems, out_sems, arrived_sem):
        def in_copy(chunk):
            place = rows_at(chunk, tile)
            return pltpu.make_async_copy(total_hbm.at[place], held.at[place], in_sems.at[chunk])

        def out_copy(chunk):
            place = rows_at(chunk, tile)
            return pltpu.make_async_copy(held.at[place], out_hbm.at[place], out_sems.at[chunk])

        arrived_copy = pltpu.make_async_copy(arrived_hbm, arrived_ref, arrived_sem)
        arrived_copy.start()
        every(chunks, lambda chunk: in_copy(chunk).start())
        arrived_copy.wait()
        peaks, masses = arrived_ref[:, 0, :], arrived_ref[:, 1, :]
        row_peak = jnp.max(peaks, axis=0, keepdims=True)
        row_mass = jnp.sum(masses * jnp.exp(peaks - row_peak), axis=0, keepdims=True)
        log_total = row_peak + jnp.log(row_mass)

        def shift(chunk):
            in_copy(chunk).wait()
            place = rows_at(chunk, tile)
            held[place, :] = held[place, :] - log_total
            out_copy(chunk).start()

        every(chunks, shift)
        every(chunks, lambda chunk: out_copy(chunk).wait())

    return pl.pallas_call(
        kernel,
        in_specs=[ANYWHERE] * 2,
        out_specs=ANYWHERE,
        out_shape=jax.ShapeDtypeStruct((vocabulary, rows), jnp.float32),
        scratch_shapes=[pltpu.VMEM((vocabulary, rows), jnp.float32), pltpu.VMEM(arrived.shape, jnp.float32)]
        + [pltpu.SemaphoreType.DMA((chunks,))] * 2
        + [pltpu.SemaphoreType.DMA],
        compiler_params=ROOM,
        cost_estimate=pl.CostEstimate(flops=vocabulary * rows, bytes_accessed=8 * vocabulary * rows, transcendentals=0),
        name="subtract",
    )(total, arrived)


def slot_factors(slot_code, slot_count):
    slots = slot_code.shape[2]
    active = jnp.arange(slots, dtype=jnp.int32)[None, None, :] < slot_count[:, :, None]
    return jnp.where(active, slot_code, 0).astype(jnp.float32) * 0.25


def body(hidden, norm_gain, head_weight, diff_rows, slot_request, slot_code, slot_count):
    me, core = lax.axis_index("wide"), lax.axis_index("narrow")
    parts, rows = lax.axis_size("wide"), hidden.shape[0]
    weight_t = head_weight.T

    def move(a, mask):
        return flip(a, "wide", mask)

    own = normalise(hidden, norm_gain)
    x0, y0, z1, z2 = move(own, 1), move(own, 2), move(own, 4), move(own, 8)
    slices = vocabulary_slices(after(diff_rows, own)[0, 0], parts)

    own, x0, y0, z1, slices = lax.optimization_barrier((own, x0, y0, z1, slices))
    x1, y1 = move(z1, 1), move(z1, 2)
    chosen = core * 8 * rows + jnp.arange(8 * rows, dtype=jnp.int32)
    factors = slot_factors(slot_code, slot_count)

    def mixing(which):
        targets = lax.dynamic_index_in_dim(slot_request, which, 1, False).reshape(-1)
        weights = lax.dynamic_index_in_dim(factors, which, 1, False).reshape(-1)
        return jnp.where(chosen[:, None] == targets, weights, 0.0).astype(jnp.bfloat16)

    mixings = [mixing(core), mixing(1 - core)]

    x1, y1, z2, y0, mixings = lax.optimization_barrier((x1, y1, z2, y0, mixings))
    d0, d1, z3 = move(y0, 1), move(x1, 2), move(z2, 4)

    d0, d1, z3, z2 = lax.optimization_barrier((d0, d1, z3, z2))
    x2, y2, x3, y3 = move(z2, 1), move(z2, 2), move(z3, 1), move(z3, 2)
    first, half = me & 7, me // 8
    late = half ^ core
    chunks = weight_t.shape[0] // tile_of(weight_t.shape[0])
    near = multiply([own, x0, y0, d0, z1, x1, y1, d1], weight_t, first, 0, chunks)

    x3, y3, y2, x2, near, slices = lax.optimization_barrier((x3, y3, y2, x2, near, slices))
    d2, d3 = move(y2, 1), move(x3, 2)
    near_other = flip(near, "narrow", 1)
    diffs = lax.all_to_all(slices, "wide", split_axis=0, concat_axis=0, tiled=True)

    d2, d3, near_other = lax.optimization_barrier((d2, d3, near_other))
    far = multiply([z2, x2, y2, d2, z3, x3, y3, d3], weight_t, first, 0, chunks)
    far, diffs = lax.optimization_barrier((far, diffs))
    far_other = flip(far, "narrow", 1)
    diffs = diffs.reshape(-1, weight_t.shape[0]).T
    diffs_other = flip(diffs, "narrow", 1)
    total, stats = statistics([near], [near_other], far, far_other, [diffs, diffs_other], mixings, late, parts)
    arrived = lax.all_to_all(stats, "wide", split_axis=0, concat_axis=0, tiled=True)
    return subtract(total, arrived).T


def combined_all(part, axis, combine):
    gathered = jax.tree.map(lambda a: lax.all_gather(a, axis), part)

    def take(source):
        return jax.tree.map(lambda a: lax.dynamic_index_in_dim(a, source, 0, False), gathered)

    return lax.fori_loop(
        1, lax.axis_size(axis), lambda source, state: combine(state, take(source)), take(0)
    )


def merge_pair(earlier, later):
    row_peak = jnp.maximum(earlier[0], later[0])
    summed = earlier[1] * jnp.exp(earlier[0] - row_peak) + later[1] * jnp.exp(later[0] - row_peak)
    return (row_peak, summed)


def general_body(hidden, norm_gain, head_weight, diff_rows, slot_request, slot_code, slot_count):
    values = hidden.astype(jnp.float32)
    squares = lax.psum(jnp.sum(values * values, axis=1), "narrow")
    scales = lax.rsqrt(squares / D + epsilon)
    normed = (values * scales[:, None] * norm_gain[None, :]).astype(jnp.bfloat16)
    partial_value = jnp.dot(
        lax.all_gather(normed, "wide", axis=0, tiled=True),
        head_weight,
        preferred_element_type=jnp.float32,
    )
    arrived = lax.all_to_all(diff_rows[0, 0], "wide", split_axis=1, concat_axis=0, tiled=True)
    base_block = lax.psum_scatter(partial_value, "narrow", scatter_dimension=0, tiled=True)
    owner_slices = lax.all_gather(arrived, "narrow", axis=0, tiled=True)
    targets = jnp.transpose(slot_request, (1, 0, 2)).reshape(-1)
    factor_all = jnp.transpose(slot_factors(slot_code, slot_count), (1, 0, 2)).reshape(-1)
    block_rows = base_block.shape[0]
    offsets = targets - lax.axis_index("narrow") * block_rows
    owned = (offsets >= 0) & (offsets < block_rows)
    factors = jnp.where(owned, factor_all, 0.0)
    target_rows = jnp.where(owned, offsets, 0)
    own_block = base_block.at[target_rows].add(owner_slices.astype(jnp.float32) * factors[:, None])
    local_peak = jnp.max(own_block, axis=1)
    local_mass = jnp.sum(jnp.exp(own_block - local_peak[:, None]), axis=1)
    row_peak, row_mass = combined_all((local_peak, local_mass), "wide", merge_pair)
    log_total = row_peak + jnp.log(row_mass)
    return own_block - log_total[:, None]


def solution(mesh):
    placed = (
        P("wide", "narrow"),
        P("narrow"),
        P("narrow", "wide"),
        P("wide", "narrow", None, None),
        P(),
        P(),
        P(),
    )
    small = mesh.shape["wide"] == 16 and mesh.shape["narrow"] == 2
    return jax.shard_map(
        body if small else general_body,
        mesh=mesh,
        in_specs=placed,
        out_specs=P("narrow", "wide"),
        check_vma=False,
    )
```

```python
import jax
import jax.numpy as jnp
from jax import lax
from jax.experimental import pallas as pl
from jax.experimental.pallas import tpu as pltpu
from jax.sharding import PartitionSpec as P

D = 8192


epsilon = 1e-05
ANYWHERE = pl.BlockSpec(memory_space=pl.ANY)
SCALAR = pl.BlockSpec(memory_space=pltpu.SMEM)
ROOM = pltpu.CompilerParams(vmem_limit_bytes=56 * 2**20)


def flip(a, axis, mask):
    size = lax.axis_size(axis)
    return lax.ppermute(a, axis, [(i, i ^ mask) for i in range(size)])


def after(a, *others):
    return lax.optimization_barrier((a, *others))[0]


def normalise(hidden, norm_gain):
    values = hidden.astype(jnp.float32)
    sums = jnp.sum(values * values, axis=1)
    squares = sums + flip(sums, "narrow", 1)
    scales = lax.rsqrt(squares / D + epsilon)
    return (values * scales[:, None] * norm_gain[None, :]).astype(jnp.bfloat16)


def vocabulary_slices(row_block, parts):
    def kernel(rows_ref, slices_ref):
        width = slices_ref.shape[2]
        for part in range(parts):
            slices_ref[part] = rows_ref[:, part * width : (part + 1) * width]

    slots, vocabulary = row_block.shape
    return pl.pallas_call(
        kernel,
        out_shape=jax.ShapeDtypeStruct((parts, slots, vocabulary // parts), row_block.dtype),
        cost_estimate=pl.CostEstimate(flops=0, bytes_accessed=4 * slots * vocabulary, transcendentals=0),
        name="vocabulary_slices",
    )(row_block)


def in_hbm(a):
    return pltpu.with_memory_space_constraint(a, pltpu.HBM)


def tile_of(length):
    return max(t for t in range(16, 513, 16) if length % t == 0)


def every(count, step):
    def loop(i, _):
        step(i)
        return 0

    lax.fori_loop(0, count, loop, 0)


def rows_at(i, tile):
    return pl.ds(pl.multiple_of(i * tile, 8), tile)


def multiply(blocks, weight_t, first, pieces):
    width = weight_t.shape[1]
    count, rows = len(blocks), blocks[0].shape[0]
    tile = tile_of(weight_t.shape[0])
    chunks = sum(pieces)
    begins = [sum(pieces[:n]) for n in range(len(pieces))]
    contract_last = (((1,), (1,)), ((), ()))

    def kernel(first_ref, *refs):
        block_refs, refs = refs[:count], refs[count:]
        weight_hbm, out_hbms, refs = refs[0], refs[1 : 1 + len(pieces)], refs[1 + len(pieces) :]
        states, weight, out, state_sems, weight_sems, out_sems = refs

        def weight_copy(chunk):
            place = rows_at(chunk, tile)
            return pltpu.make_async_copy(weight_hbm.at[place], weight.at[place], weight_sems.at[chunk])

        def out_copy(piece, chunk):
            source = out.at[rows_at(begins[piece] + chunk, tile)]
            target = out_hbms[piece].at[rows_at(chunk, tile)]
            return pltpu.make_async_copy(source, target, out_sems.at[begins[piece] + chunk])

        def one_chunk(chunk):
            weight_copy(chunk).wait()
            place = rows_at(chunk, tile)
            out[place, :] = lax.dot_general(
                weight[place, :], states[...], contract_last, preferred_element_type=jnp.float32
            )
            for piece, (begin, length) in enumerate(zip(begins, pieces)):

                @pl.when((chunk >= begin) & (chunk < begin + length))
                def _():
                    out_copy(piece, chunk - begin).start()

        state_copies = [
            pltpu.make_async_copy(
                block_refs[k],
                states.at[pl.ds(pl.multiple_of((first_ref[0] ^ k) * rows, rows), rows)],
                state_sems.at[k],
            )
            for k in range(count)
        ]
        for copy in state_copies:
            copy.start()
        every(chunks, lambda chunk: weight_copy(chunk).start())
        for copy in state_copies:
            copy.wait()
        every(chunks, one_chunk)
        for piece, length in enumerate(pieces):
            every(length, lambda chunk, piece=piece: out_copy(piece, chunk).wait())

    return pl.pallas_call(
        kernel,
        in_specs=[SCALAR] + [ANYWHERE] * (count + 1),
        out_specs=[ANYWHERE] * len(pieces),
        out_shape=[jax.ShapeDtypeStruct((length * tile, count * rows), jnp.float32) for length in pieces],
        scratch_shapes=[
            pltpu.VMEM((count * rows, width), jnp.bfloat16),
            pltpu.VMEM((chunks * tile, width), jnp.bfloat16),
            pltpu.VMEM((chunks * tile, count * rows), jnp.float32),
            pltpu.SemaphoreType.DMA((count,)),
            pltpu.SemaphoreType.DMA((chunks,)),
            pltpu.SemaphoreType.DMA((chunks,)),
        ],
        compiler_params=ROOM,
        cost_estimate=pl.CostEstimate(
            flops=8 * chunks * tile * width * count * rows, bytes_accessed=8 * chunks * tile * width, transcendentals=0
        ),
        name="multiply",
    )(first.reshape(1), *blocks, weight_t)


def statistics(near, near_other, far, far_other, diffs, mixing, late, parts):
    vocabulary, rows = near.shape
    slots = diffs[0].shape[1]
    tile = tile_of(vocabulary)
    chunks = vocabulary // tile
    pieces = len(far)
    contract_last = (((1,), (1,)), ((), ()))

    def kernel(late_ref, *refs):
        near_ref, near_other_ref, *refs = refs
        far_refs, far_other_refs, refs = refs[:pieces], refs[pieces : 2 * pieces], refs[2 * pieces :]
        diff_refs, mixing_refs, refs = refs[:2], refs[2:4], refs[4:]
        total_hbm, stats_ref, left, right, rows_in, mixed, left_sems, right_sems, out_sems, side_sems = refs

        def fetch(chunk, source, left_side, right_side):
            origin, place = rows_at(source, tile), rows_at(chunk, tile)
            return [
                pltpu.make_async_copy(left_side.at[origin], left.at[place], left_sems.at[chunk]),
                pltpu.make_async_copy(right_side.at[origin], right.at[place], right_sems.at[chunk]),
            ]

        def out_copy(chunk):
            place = rows_at(chunk, tile)
            return pltpu.make_async_copy(left.at[place], total_hbm.at[place], out_sems.at[chunk])

        def start_all(first, left_side, right_side):
            def start(chunk):
                for copy in fetch(first + chunk, chunk, left_side, right_side):
                    copy.start()

            every(left_side.shape[0] // tile, start)

        side_copies = [
            pltpu.make_async_copy(source, into.at[:, pl.ds(n * slots, slots)], side_sems.at[side, n])
            for side, (sources, into) in enumerate(((mixing_refs, mixed), (diff_refs, rows_in)))
            for n, source in enumerate(sources)
        ]
        for copy in side_copies:
            copy.start()

        @pl.when(late_ref[0] == 0)
        def _():
            start_all(0, near_ref, near_other_ref)

        @pl.when(late_ref[0] == 1)
        def _():
            first = 0
            for left_side, right_side in zip(far_refs, far_other_refs):
                start_all(first, left_side, right_side)
                first += left_side.shape[0] // tile

        for copy in side_copies:
            copy.wait()

        def step(chunk, state):
            for copy in fetch(chunk, chunk, near_ref, near_other_ref):
                copy.wait()
            place = rows_at(chunk, tile)
            total = left[place, :] + right[place, :]
            total += lax.dot_general(
                rows_in[place, :], mixed[...], contract_last, preferred_element_type=jnp.float32
            )
            left[place, :] = total
            out_copy(chunk).start()
            before, mass = state
            peak = jnp.maximum(before, jnp.max(total, axis=0, keepdims=True))
            total = left[place, :]
            mass = mass * jnp.exp(before - peak) + jnp.sum(jnp.exp(total - peak), axis=0, keepdims=True)
            return peak, mass

        state = (jnp.full((1, rows), -jnp.inf, jnp.float32), jnp.zeros((1, rows), jnp.float32))
        both = jnp.concatenate(lax.fori_loop(0, chunks, step, state))
        stats_ref[...] = jnp.broadcast_to(both[None], stats_ref.shape)
        every(chunks, lambda chunk: out_copy(chunk).wait())

    return pl.pallas_call(
        kernel,
        in_specs=[SCALAR] + [ANYWHERE] * (2 * pieces + 6),
        out_specs=[ANYWHERE, pl.BlockSpec(memory_space=pltpu.VMEM)],
        out_shape=[
            jax.ShapeDtypeStruct((vocabulary, rows), jnp.float32),
            jax.ShapeDtypeStruct((parts, 2, rows), jnp.float32),
        ],
        scratch_shapes=[pltpu.VMEM((vocabulary, rows), jnp.float32)] * 2
        + [pltpu.VMEM((vocabulary, 2 * slots), jnp.bfloat16), pltpu.VMEM((rows, 2 * slots), jnp.bfloat16)]
        + [pltpu.SemaphoreType.DMA((chunks,))] * 3
        + [pltpu.SemaphoreType.DMA((2, 2))],
        compiler_params=pltpu.CompilerParams(vmem_limit_bytes=12 * 2**20),
        cost_estimate=pl.CostEstimate(
            flops=4 * vocabulary * rows, bytes_accessed=16 * vocabulary * rows, transcendentals=vocabulary * rows
        ),
        name="statistics",
    )(late.reshape(1), in_hbm(near), in_hbm(near_other), *map(in_hbm, far), *far_other, *diffs, *mixing)


def subtract(total, arrived):
    vocabulary, rows = total.shape
    tile = tile_of(vocabulary)
    chunks = vocabulary // tile

    def kernel(total_hbm, arrived_hbm, out_hbm, held, arrived_ref, in_sems, out_sems, arrived_sem):
        def in_copy(chunk):
            place = rows_at(chunk, tile)
            return pltpu.make_async_copy(total_hbm.at[place], held.at[place], in_sems.at[chunk])

        def out_copy(chunk):
            place = rows_at(chunk, tile)
            return pltpu.make_async_copy(held.at[place], out_hbm.at[place], out_sems.at[chunk])

        arrived_copy = pltpu.make_async_copy(arrived_hbm, arrived_ref, arrived_sem)
        arrived_copy.start()
        every(chunks, lambda chunk: in_copy(chunk).start())
        arrived_copy.wait()
        peaks, masses = arrived_ref[:, 0, :], arrived_ref[:, 1, :]
        row_peak = jnp.max(peaks, axis=0, keepdims=True)
        row_mass = jnp.sum(masses * jnp.exp(peaks - row_peak), axis=0, keepdims=True)
        log_total = row_peak + jnp.log(row_mass)

        def shift(chunk):
            in_copy(chunk).wait()
            place = rows_at(chunk, tile)
            held[place, :] = held[place, :] - log_total
            out_copy(chunk).start()

        every(chunks, shift)
        every(chunks, lambda chunk: out_copy(chunk).wait())

    return pl.pallas_call(
        kernel,
        in_specs=[ANYWHERE] * 2,
        out_specs=ANYWHERE,
        out_shape=jax.ShapeDtypeStruct((vocabulary, rows), jnp.float32),
        scratch_shapes=[pltpu.VMEM((vocabulary, rows), jnp.float32), pltpu.VMEM(arrived.shape, jnp.float32)]
        + [pltpu.SemaphoreType.DMA((chunks,))] * 2
        + [pltpu.SemaphoreType.DMA],
        compiler_params=pltpu.CompilerParams(vmem_limit_bytes=12 * 2**20),
        cost_estimate=pl.CostEstimate(flops=vocabulary * rows, bytes_accessed=8 * vocabulary * rows, transcendentals=0),
        name="subtract",
    )(total, arrived)


def slot_factors(slot_code, slot_count):
    slots = slot_code.shape[2]
    active = jnp.arange(slots, dtype=jnp.int32)[None, None, :] < slot_count[:, :, None]
    return jnp.where(active, slot_code, 0).astype(jnp.float32) * 0.25


def body(hidden, norm_gain, head_weight, diff_rows, slot_request, slot_code, slot_count):
    me, core = lax.axis_index("wide"), lax.axis_index("narrow")
    parts, rows = lax.axis_size("wide"), hidden.shape[0]
    weight_t = head_weight.T

    def move(a, mask):
        return flip(a, "wide", mask)

    own = normalise(hidden, norm_gain)
    x0, y0, z1, z2 = move(own, 1), move(own, 2), move(own, 4), move(own, 8)
    slices = vocabulary_slices(after(diff_rows, own)[0, 0], parts)

    chosen = core * 8 * rows + jnp.arange(8 * rows, dtype=jnp.int32)
    factors = slot_factors(slot_code, slot_count)

    def mixing(which):
        targets = lax.dynamic_index_in_dim(slot_request, which, 1, False).reshape(-1)
        weights = lax.dynamic_index_in_dim(factors, which, 1, False).reshape(-1)
        return jnp.where(chosen[:, None] == targets, weights, 0.0).astype(jnp.bfloat16)

    mixings = [mixing(core), mixing(1 - core)]

    own, x0, y0, z1, slices, mixings = lax.optimization_barrier((own, x0, y0, z1, slices, mixings))
    x1, y1, d0 = move(z1, 1), move(z1, 2), move(y0, 1)

    x1, z2 = lax.optimization_barrier((x1, z2))
    d1, z3 = move(x1, 2), move(z2, 4)

    d0, y1, z2 = lax.optimization_barrier((d0, y1, z2))
    x2, y2 = move(z2, 1), move(z2, 2)
    d1, z3 = lax.optimization_barrier((d1, z3))
    x3, y3 = move(z3, 1), move(z3, 2)
    first, half = me & 7, me // 8
    late = half ^ core
    chunks = weight_t.shape[0] // tile_of(weight_t.shape[0])
    (near,) = multiply([own, x0, y0, d0, z1, x1, y1, d1], weight_t, first, [chunks])

    x3, y3, y2, x2, near, slices = lax.optimization_barrier((x3, y3, y2, x2, near, slices))
    d2, d3 = move(y2, 1), move(x3, 2)
    near_other = flip(near, "narrow", 1)
    diffs = lax.all_to_all(slices, "wide", split_axis=0, concat_axis=0, tiled=True)

    d2, d3, near_other = lax.optimization_barrier((d2, d3, near_other))
    middle = (chunks + 1) // 2
    far = list(multiply([z2, x2, y2, d2, z3, x3, y3, d3], weight_t, first, [middle, chunks - middle]))
    far_other = [flip(far[0], "narrow", 1)]
    far[1], diffs = lax.optimization_barrier((far[1], diffs))
    far_other.append(flip(far[1], "narrow", 1))
    diffs = diffs.reshape(-1, weight_t.shape[0])
    diffs, diffs_other = diffs.T, flip(diffs, "narrow", 1).T
    total, stats = statistics(near, near_other, far, far_other, [diffs, diffs_other], mixings, late, parts)
    arrived = lax.all_to_all(stats, "wide", split_axis=0, concat_axis=0, tiled=True)
    return subtract(total, arrived).T


def combined_all(part, axis, combine):
    gathered = jax.tree.map(lambda a: lax.all_gather(a, axis), part)

    def take(source):
        return jax.tree.map(lambda a: lax.dynamic_index_in_dim(a, source, 0, False), gathered)

    return lax.fori_loop(
        1, lax.axis_size(axis), lambda source, state: combine(state, take(source)), take(0)
    )


def merge_pair(earlier, later):
    row_peak = jnp.maximum(earlier[0], later[0])
    summed = earlier[1] * jnp.exp(earlier[0] - row_peak) + later[1] * jnp.exp(later[0] - row_peak)
    return (row_peak, summed)


def general_body(hidden, norm_gain, head_weight, diff_rows, slot_request, slot_code, slot_count):
    values = hidden.astype(jnp.float32)
    squares = lax.psum(jnp.sum(values * values, axis=1), "narrow")
    scales = lax.rsqrt(squares / D + epsilon)
    normed = (values * scales[:, None] * norm_gain[None, :]).astype(jnp.bfloat16)
    partial_value = jnp.dot(
        lax.all_gather(normed, "wide", axis=0, tiled=True),
        head_weight,
        preferred_element_type=jnp.float32,
    )
    arrived = lax.all_to_all(diff_rows[0, 0], "wide", split_axis=1, concat_axis=0, tiled=True)
    base_block = lax.psum_scatter(partial_value, "narrow", scatter_dimension=0, tiled=True)
    owner_slices = lax.all_gather(arrived, "narrow", axis=0, tiled=True)
    targets = jnp.transpose(slot_request, (1, 0, 2)).reshape(-1)
    factor_all = jnp.transpose(slot_factors(slot_code, slot_count), (1, 0, 2)).reshape(-1)
    block_rows = base_block.shape[0]
    offsets = targets - lax.axis_index("narrow") * block_rows
    owned = (offsets >= 0) & (offsets < block_rows)
    factors = jnp.where(owned, factor_all, 0.0)
    target_rows = jnp.where(owned, offsets, 0)
    own_block = base_block.at[target_rows].add(owner_slices.astype(jnp.float32) * factors[:, None])
    local_peak = jnp.max(own_block, axis=1)
    local_mass = jnp.sum(jnp.exp(own_block - local_peak[:, None]), axis=1)
    row_peak, row_mass = combined_all((local_peak, local_mass), "wide", merge_pair)
    log_total = row_peak + jnp.log(row_mass)
    return own_block - log_total[:, None]


def solution(mesh):
    placed = (
        P("wide", "narrow"),
        P("narrow"),
        P("narrow", "wide"),
        P("wide", "narrow", None, None),
        P(),
        P(),
        P(),
    )
    small = mesh.shape["wide"] == 16 and mesh.shape["narrow"] == 2
    return jax.shard_map(
        body if small else general_body,
        mesh=mesh,
        in_specs=placed,
        out_specs=P("narrow", "wide"),
        check_vma=False,
    )
```

```python
import jax
import jax.numpy as jnp
from jax import lax
from jax.experimental import pallas as pl
from jax.experimental.pallas import tpu as pltpu
from jax.sharding import PartitionSpec as P

D = 8192


epsilon = 1e-05
ANYWHERE = pl.BlockSpec(memory_space=pl.ANY)
SCALAR = pl.BlockSpec(memory_space=pltpu.SMEM)
ROOM = pltpu.CompilerParams(vmem_limit_bytes=46 * 2**20)


def flip(a, axis, mask):
    size = lax.axis_size(axis)
    return lax.ppermute(a, axis, [(i, i ^ mask) for i in range(size)])


def after(a, *others):
    return lax.optimization_barrier((a, *others))[0]


def normalise(hidden, norm_gain):
    values = hidden.astype(jnp.float32)
    sums = jnp.sum(values * values, axis=1)
    squares = sums + flip(sums, "narrow", 1)
    scales = lax.rsqrt(squares / D + epsilon)
    return (values * scales[:, None] * norm_gain[None, :]).astype(jnp.bfloat16)


def vocabulary_slices(row_block, parts):
    def kernel(rows_ref, slices_ref):
        width = slices_ref.shape[2]
        for part in range(parts):
            slices_ref[part] = rows_ref[:, part * width : (part + 1) * width]

    slots, vocabulary = row_block.shape
    return pl.pallas_call(
        kernel,
        out_shape=jax.ShapeDtypeStruct((parts, slots, vocabulary // parts), row_block.dtype),
        cost_estimate=pl.CostEstimate(flops=0, bytes_accessed=4 * slots * vocabulary, transcendentals=0),
        name="vocabulary_slices",
    )(row_block)


def in_hbm(a):
    return pltpu.with_memory_space_constraint(a, pltpu.HBM)


def tile_of(length):
    return max(t for t in range(16, 513, 16) if length % t == 0)


def every(count, step):
    def loop(i, _):
        step(i)
        return 0

    lax.fori_loop(0, count, loop, 0)


def rows_at(i, tile):
    return pl.ds(pl.multiple_of(i * tile, 8), tile)


def multiply(blocks, fresh, weight_t, first, pieces):
    width = weight_t.shape[1]
    count, rows = len(blocks), blocks[0].shape[0]
    tile = tile_of(weight_t.shape[0])
    chunks = sum(pieces)
    begins = [sum(pieces[:n]) for n in range(len(pieces))]
    contract_last = (((1,), (1,)), ((), ()))

    def kernel(first_ref, *refs):
        block_refs, refs = refs[:count], refs[count:]
        weight_hbm, out_hbms, refs = refs[0], refs[1 : 1 + len(pieces)], refs[1 + len(pieces) :]
        states, weight, out, state_sems, weight_sems, out_sems = refs

        def weight_copy(chunk):
            place = rows_at(chunk, tile)
            return pltpu.make_async_copy(weight_hbm.at[place], weight.at[place], weight_sems.at[chunk])

        def out_copy(piece, chunk):
            source = out.at[rows_at(begins[piece] + chunk, tile)]
            target = out_hbms[piece].at[rows_at(chunk, tile)]
            return pltpu.make_async_copy(source, target, out_sems.at[begins[piece] + chunk])

        def one_chunk(chunk):
            weight_copy(chunk).wait()
            place = rows_at(chunk, tile)
            out[place, :] = lax.dot_general(
                weight[place, :], states[...], contract_last, preferred_element_type=jnp.float32
            )
            for piece, (begin, length) in enumerate(zip(begins, pieces)):

                @pl.when((chunk >= begin) & (chunk < begin + length))
                def _():
                    out_copy(piece, chunk - begin).start()

        state_copies = [
            pltpu.make_async_copy(
                block_refs[k],
                states.at[pl.ds(pl.multiple_of((first_ref[0] ^ k) * rows, rows), rows)],
                state_sems.at[k],
            )
            for k in range(count)
        ]
        for copy in state_copies:
            copy.start()
        every(chunks, lambda chunk: weight_copy(chunk).start())
        for copy in state_copies:
            copy.wait()
        every(chunks, one_chunk)
        for piece, length in enumerate(pieces):
            every(length, lambda chunk, piece=piece: out_copy(piece, chunk).wait())

    return pl.pallas_call(
        kernel,
        in_specs=[SCALAR] + [ANYWHERE] * (count + 1),
        out_specs=[ANYWHERE] * len(pieces),
        out_shape=[jax.ShapeDtypeStruct((length * tile, count * rows), jnp.float32) for length in pieces],
        scratch_shapes=[
            pltpu.VMEM((count * rows, width), jnp.bfloat16),
            pltpu.VMEM((chunks * tile, width), jnp.bfloat16),
            pltpu.VMEM((chunks * tile, count * rows), jnp.float32),
            pltpu.SemaphoreType.DMA((count,)),
            pltpu.SemaphoreType.DMA((chunks,)),
            pltpu.SemaphoreType.DMA((chunks,)),
        ],
        compiler_params=ROOM,
        cost_estimate=pl.CostEstimate(
            flops=8 * chunks * tile * width * count * rows, bytes_accessed=8 * chunks * tile * width, transcendentals=0
        ),
        name="multiply",
    )(first.reshape(1), *(a if n in fresh else in_hbm(a) for n, a in enumerate(blocks)), in_hbm(weight_t))


def statistics(near, near_other, far, far_other, diffs, mixing, late, parts):
    vocabulary, rows = near.shape
    slots = diffs[0].shape[1]
    tile = tile_of(vocabulary)
    chunks = vocabulary // tile
    pieces = len(far)
    contract_last = (((1,), (1,)), ((), ()))

    def kernel(late_ref, *refs):
        near_ref, near_other_ref, *refs = refs
        far_refs, far_other_refs, refs = refs[:pieces], refs[pieces : 2 * pieces], refs[2 * pieces :]
        diff_refs, mixing_refs, refs = refs[:2], refs[2:4], refs[4:]
        total_hbm, stats_ref, left, right, rows_in, mixed, left_sems, right_sems, out_sems, side_sems = refs

        def fetch(chunk, source, left_side, right_side):
            origin, place = rows_at(source, tile), rows_at(chunk, tile)
            return [
                pltpu.make_async_copy(left_side.at[origin], left.at[place], left_sems.at[chunk]),
                pltpu.make_async_copy(right_side.at[origin], right.at[place], right_sems.at[chunk]),
            ]

        def out_copy(chunk):
            place = rows_at(chunk, tile)
            return pltpu.make_async_copy(left.at[place], total_hbm.at[place], out_sems.at[chunk])

        def start_all(first, left_side, right_side):
            def start(chunk):
                for copy in fetch(first + chunk, chunk, left_side, right_side):
                    copy.start()

            every(left_side.shape[0] // tile, start)

        side_copies = [
            pltpu.make_async_copy(source, into.at[:, pl.ds(n * slots, slots)], side_sems.at[side, n])
            for side, (sources, into) in enumerate(((mixing_refs, mixed), (diff_refs, rows_in)))
            for n, source in enumerate(sources)
        ]
        for copy in side_copies:
            copy.start()

        @pl.when(late_ref[0] == 0)
        def _():
            start_all(0, near_ref, near_other_ref)

        @pl.when(late_ref[0] == 1)
        def _():
            first = 0
            for left_side, right_side in zip(far_refs, far_other_refs):
                start_all(first, left_side, right_side)
                first += left_side.shape[0] // tile

        for copy in side_copies:
            copy.wait()

        def step(chunk, state):
            for copy in fetch(chunk, chunk, near_ref, near_other_ref):
                copy.wait()
            place = rows_at(chunk, tile)
            total = left[place, :] + right[place, :]
            total += lax.dot_general(
                rows_in[place, :], mixed[...], contract_last, preferred_element_type=jnp.float32
            )
            left[place, :] = total
            out_copy(chunk).start()
            before, mass = state
            peak = jnp.maximum(before, jnp.max(total, axis=0, keepdims=True))
            total = left[place, :]
            mass = mass * jnp.exp(before - peak) + jnp.sum(jnp.exp(total - peak), axis=0, keepdims=True)
            return peak, mass

        state = (jnp.full((1, rows), -jnp.inf, jnp.float32), jnp.zeros((1, rows), jnp.float32))
        both = jnp.concatenate(lax.fori_loop(0, chunks, step, state))
        stats_ref[...] = jnp.broadcast_to(both[None], stats_ref.shape)
        every(chunks, lambda chunk: out_copy(chunk).wait())

    return pl.pallas_call(
        kernel,
        in_specs=[SCALAR] + [ANYWHERE] * (2 * pieces + 6),
        out_specs=[ANYWHERE, pl.BlockSpec(memory_space=pltpu.VMEM)],
        out_shape=[
            jax.ShapeDtypeStruct((vocabulary, rows), jnp.float32),
            jax.ShapeDtypeStruct((parts, 2, rows), jnp.float32),
        ],
        scratch_shapes=[pltpu.VMEM((vocabulary, rows), jnp.float32)] * 2
        + [pltpu.VMEM((vocabulary, 2 * slots), jnp.bfloat16), pltpu.VMEM((rows, 2 * slots), jnp.bfloat16)]
        + [pltpu.SemaphoreType.DMA((chunks,))] * 3
        + [pltpu.SemaphoreType.DMA((2, 2))],
        compiler_params=pltpu.CompilerParams(vmem_limit_bytes=12 * 2**20),
        cost_estimate=pl.CostEstimate(
            flops=4 * vocabulary * rows, bytes_accessed=16 * vocabulary * rows, transcendentals=vocabulary * rows
        ),
        name="statistics",
    )(late.reshape(1), in_hbm(near), in_hbm(near_other), *map(in_hbm, far), *far_other, *diffs, *mixing)


def subtract(total, arrived):
    vocabulary, rows = total.shape
    tile = tile_of(vocabulary)
    chunks = vocabulary // tile

    def kernel(total_hbm, arrived_hbm, out_hbm, held, arrived_ref, in_sems, out_sems, arrived_sem):
        def in_copy(chunk):
            place = rows_at(chunk, tile)
            return pltpu.make_async_copy(total_hbm.at[place], held.at[place], in_sems.at[chunk])

        def out_copy(chunk):
            place = rows_at(chunk, tile)
            return pltpu.make_async_copy(held.at[place], out_hbm.at[place], out_sems.at[chunk])

        arrived_copy = pltpu.make_async_copy(arrived_hbm, arrived_ref, arrived_sem)
        arrived_copy.start()
        every(chunks, lambda chunk: in_copy(chunk).start())
        arrived_copy.wait()
        peaks, masses = arrived_ref[:, 0, :], arrived_ref[:, 1, :]
        row_peak = jnp.max(peaks, axis=0, keepdims=True)
        row_mass = jnp.sum(masses * jnp.exp(peaks - row_peak), axis=0, keepdims=True)
        log_total = row_peak + jnp.log(row_mass)

        def shift(chunk):
            in_copy(chunk).wait()
            place = rows_at(chunk, tile)
            held[place, :] = held[place, :] - log_total
            out_copy(chunk).start()

        every(chunks, shift)
        every(chunks, lambda chunk: out_copy(chunk).wait())

    return pl.pallas_call(
        kernel,
        in_specs=[ANYWHERE] * 2,
        out_specs=ANYWHERE,
        out_shape=jax.ShapeDtypeStruct((vocabulary, rows), jnp.float32),
        scratch_shapes=[pltpu.VMEM((vocabulary, rows), jnp.float32), pltpu.VMEM(arrived.shape, jnp.float32)]
        + [pltpu.SemaphoreType.DMA((chunks,))] * 2
        + [pltpu.SemaphoreType.DMA],
        compiler_params=pltpu.CompilerParams(vmem_limit_bytes=12 * 2**20),
        cost_estimate=pl.CostEstimate(flops=vocabulary * rows, bytes_accessed=8 * vocabulary * rows, transcendentals=0),
        name="subtract",
    )(total, arrived)


def slot_factors(slot_code, slot_count):
    slots = slot_code.shape[2]
    active = jnp.arange(slots, dtype=jnp.int32)[None, None, :] < slot_count[:, :, None]
    return jnp.where(active, slot_code, 0).astype(jnp.float32) * 0.25


def body(hidden, norm_gain, head_weight, diff_rows, slot_request, slot_code, slot_count):
    me, core = lax.axis_index("wide"), lax.axis_index("narrow")
    parts, rows = lax.axis_size("wide"), hidden.shape[0]
    weight_t = head_weight.T

    def move(a, mask):
        return flip(a, "wide", mask)

    own = normalise(hidden, norm_gain)
    x0, y0, z1, z2 = move(own, 1), move(own, 2), move(own, 4), move(own, 8)
    slices = vocabulary_slices(after(diff_rows, own)[0, 0], parts)

    chosen = core * 8 * rows + jnp.arange(8 * rows, dtype=jnp.int32)
    factors = slot_factors(slot_code, slot_count)

    def mixing(which):
        targets = lax.dynamic_index_in_dim(slot_request, which, 1, False).reshape(-1)
        weights = lax.dynamic_index_in_dim(factors, which, 1, False).reshape(-1)
        return jnp.where(chosen[:, None] == targets, weights, 0.0).astype(jnp.bfloat16)

    mixings = [mixing(core), mixing(1 - core)]

    own, x0, y0, z1, slices, mixings = lax.optimization_barrier((own, x0, y0, z1, slices, mixings))
    x1, y1, d0 = move(z1, 1), move(z1, 2), move(y0, 1)

    x1, z2 = lax.optimization_barrier((x1, z2))
    d1, z3 = move(x1, 2), move(z2, 4)

    d0, y1, z2 = lax.optimization_barrier((d0, y1, z2))
    x2, y2 = move(z2, 1), move(z2, 2)
    d1, z3 = lax.optimization_barrier((d1, z3))
    x3, y3 = move(z3, 1), move(z3, 2)
    first, half = me & 7, me // 8
    late = half ^ core
    chunks = weight_t.shape[0] // tile_of(weight_t.shape[0])
    (near,) = multiply([own, x0, y0, d0, z1, x1, y1, d1], [7], weight_t, first, [chunks])

    x3, y3, y2, x2, near, slices = lax.optimization_barrier((x3, y3, y2, x2, near, slices))
    d2, d3 = move(y2, 1), move(x3, 2)
    near_other = flip(near, "narrow", 1)
    diffs = lax.all_to_all(slices, "wide", split_axis=0, concat_axis=0, tiled=True)

    d2, d3, near_other = lax.optimization_barrier((d2, d3, near_other))
    middle = (chunks + 1) // 2
    far = list(multiply([z2, x2, y2, d2, z3, x3, y3, d3], [3, 7], weight_t, first, [middle, chunks - middle]))
    far_other = [flip(far[0], "narrow", 1)]
    far[1], diffs = lax.optimization_barrier((far[1], diffs))
    far_other.append(flip(far[1], "narrow", 1))
    diffs = diffs.reshape(-1, weight_t.shape[0])
    diffs, diffs_other = diffs.T, flip(diffs, "narrow", 1).T
    total, stats = statistics(near, near_other, far, far_other, [diffs, diffs_other], mixings, late, parts)
    arrived = lax.all_to_all(stats, "wide", split_axis=0, concat_axis=0, tiled=True)
    return subtract(total, arrived).T


def combined_all(part, axis, combine):
    gathered = jax.tree.map(lambda a: lax.all_gather(a, axis), part)

    def take(source):
        return jax.tree.map(lambda a: lax.dynamic_index_in_dim(a, source, 0, False), gathered)

    return lax.fori_loop(
        1, lax.axis_size(axis), lambda source, state: combine(state, take(source)), take(0)
    )


def merge_pair(earlier, later):
    row_peak = jnp.maximum(earlier[0], later[0])
    summed = earlier[1] * jnp.exp(earlier[0] - row_peak) + later[1] * jnp.exp(later[0] - row_peak)
    return (row_peak, summed)


def general_body(hidden, norm_gain, head_weight, diff_rows, slot_request, slot_code, slot_count):
    values = hidden.astype(jnp.float32)
    squares = lax.psum(jnp.sum(values * values, axis=1), "narrow")
    scales = lax.rsqrt(squares / D + epsilon)
    normed = (values * scales[:, None] * norm_gain[None, :]).astype(jnp.bfloat16)
    partial_value = jnp.dot(
        lax.all_gather(normed, "wide", axis=0, tiled=True),
        head_weight,
        preferred_element_type=jnp.float32,
    )
    arrived = lax.all_to_all(diff_rows[0, 0], "wide", split_axis=1, concat_axis=0, tiled=True)
    base_block = lax.psum_scatter(partial_value, "narrow", scatter_dimension=0, tiled=True)
    owner_slices = lax.all_gather(arrived, "narrow", axis=0, tiled=True)
    targets = jnp.transpose(slot_request, (1, 0, 2)).reshape(-1)
    factor_all = jnp.transpose(slot_factors(slot_code, slot_count), (1, 0, 2)).reshape(-1)
    block_rows = base_block.shape[0]
    offsets = targets - lax.axis_index("narrow") * block_rows
    owned = (offsets >= 0) & (offsets < block_rows)
    factors = jnp.where(owned, factor_all, 0.0)
    target_rows = jnp.where(owned, offsets, 0)
    own_block = base_block.at[target_rows].add(owner_slices.astype(jnp.float32) * factors[:, None])
    local_peak = jnp.max(own_block, axis=1)
    local_mass = jnp.sum(jnp.exp(own_block - local_peak[:, None]), axis=1)
    row_peak, row_mass = combined_all((local_peak, local_mass), "wide", merge_pair)
    log_total = row_peak + jnp.log(row_mass)
    return own_block - log_total[:, None]


def solution(mesh):
    placed = (
        P("wide", "narrow"),
        P("narrow"),
        P("narrow", "wide"),
        P("wide", "narrow", None, None),
        P(),
        P(),
        P(),
    )
    small = mesh.shape["wide"] == 16 and mesh.shape["narrow"] == 2
    return jax.shard_map(
        body if small else general_body,
        mesh=mesh,
        in_specs=placed,
        out_specs=P("narrow", "wide"),
        check_vma=False,
    )
```
